256 devices in a mesh: ctx: 32 (over z, x), head: 8 (over y, core).
Axes of the slice: x: 4, y: 4, z: 8, core: 2. Of those that a mesh axis runs over, the one named last changes fastest.
Arguments:
- queries: bfloat16 [16384, 2048], P('ctx', 'head'), may hold values from -6 to 6
- keys: bfloat16 [16384, 2048], P('ctx', 'head'), may hold values from -6 to 6
- values: bfloat16 [16384, 2048], P('ctx', 'head'), may hold values from -6 to 6
- frame_ids: int32 [64], replicated, may hold values from 0 to 31, never falling along the last dimension, each value on 1 to 4 neighbouring positions
- half_order: int32 [64], replicated, may hold values from 0 to 63, as said below
- out_weight: bfloat16 [2048, 4096], P('head'), may hold values from -0.125 to 0.125
Outputs:
- mixed: bfloat16 [16384, 4096], P('ctx', 'head')
The draws below stay inside these ranges and needn't reach their ends.
Inputs may be any that keep to these rules, and one draw needn't show every extreme that they name: `frame_ids`: never falling along the sequence; every frame number is used, by 1 to 4 blocks, and some frame by exactly 4. `half_order`: each half number appears once; device c of ctx stores halves 2 * c and 2 * c + 1; half 2 * c holds a sequence half below 32 and half 2 * c + 1 holds its mirror, 63 minus it.
All inputs are finite; a program needn't handle non-finite values.
Results may differ from the reference program's by a relative error of at most 0.02.
Values may be sent and summed in bfloat16 or wider, within the bound.
A program may use at most 128 MiB of HBM per device.

```python
import math
import jax
import jax.numpy as jnp
import numpy as np
from jax import lax

D = 4096
HD = 128
HEADS = 16
BLOCK = 256
TOK_DEV = 512
TOKENS = 16384
NBLK = 64
HALVES = 64


def draw_queries(key, part):
    key = jax.random.fold_in(key, 5)
    result = jnp.clip(jax.random.normal(key, (TOKENS, HEADS * HD), jnp.float32), -6.0, 6.0)
    return result.astype(jnp.bfloat16)


def draw_keys(key, part):
    key = jax.random.fold_in(key, 7)
    result = jnp.clip(jax.random.normal(key, (TOKENS, HEADS * HD), jnp.float32), -6.0, 6.0)
    return result.astype(jnp.bfloat16)


def draw_half_order(key, part):
    key = jax.random.fold_in(key, 11)
    lower = jax.random.permutation(key, HALVES // 2).astype(jnp.int32)
    upper = (HALVES - 1 - lower).astype(jnp.int32)
    return jnp.stack([lower, upper], axis=1).reshape(HALVES).astype(jnp.int32)


def levels(stream_key, dims, shards, smallest, top_value):
    level, own = 1.0, jax.random.fold_in(stream_key, 6)
    for dim, blocks in shards:
        draws = jnp.exp(jax.random.uniform(jax.random.fold_in(own, dim), (blocks,), jnp.float32, smallest / len(shards), top_value / len(shards)))
        level = level * jnp.repeat(draws, dims[dim] // blocks).reshape([-1 if axis == dim else 1 for axis in range(len(dims))])
    return level


def split_up(number_of, total, bound, skew):
    loads = [(1 << 20) // math.isqrt(grade ** skew) + 1 for grade in range(2, number_of + 1)]
    rest, given = total - bound - (number_of - 1), [1] * (number_of - 1)
    while rest > 0:
        free = [i for i in range(number_of - 1) if given[i] < bound]
        mass, left = sum([loads[i] for i in free]), rest
        for i in free:
            addition = min(bound - given[i], max(1, left * loads[i] // mass), rest)
            given[i] = given[i] + addition
            rest = rest - addition
    return np.array([bound] + given)


def uneven(key, number_of, total, bound, lean):
    if number_of == 2:
        one = jax.random.randint(key, (), max(1, total - bound), min(bound, total - 1) + 1)
        return jnp.stack([one, total - one])
    lengths = jnp.asarray(split_up(number_of, total, bound, lean), jnp.int32)
    couples = (number_of - 1) // 2
    donor, taker = lengths[1:1 + 2 * couples:2], lengths[2:2 + 2 * couples:2]
    room = jnp.minimum(donor - 1, bound - taker)
    shifted = jax.random.randint(jax.random.fold_in(key, 1), (couples,), 0, 1 << 20) % (room + 1)
    lengths = lengths.at[1:1 + 2 * couples:2].set(donor - shifted).at[2:2 + 2 * couples:2].set(taker + shifted)
    return lengths[jax.random.permutation(jax.random.fold_in(key, 2), number_of)]


def centred(rng, extent, deviation, reach, cuts=(), held_as=jnp.bfloat16):
    values = deviation * jax.random.normal(rng, extent, jnp.float32)
    if cuts:
        values = values * levels(rng, extent, cuts, -0.22, 0.18)
    return jnp.clip(values, -reach, reach).astype(held_as)


def setup_inputs(seed: int = 0) -> dict:
    arg_keys = jax.random.split(jax.random.key(seed), 7)
    return {
        "queries": draw_queries(jax.random.fold_in(arg_keys[6], 71), 0),
        "keys": draw_keys(jax.random.fold_in(arg_keys[6], 71), 0),
        "values": centred(arg_keys[2], (TOKENS, HEADS * HD), 1.0, 6.0, ((0, 32), (1, 8))),
        "frame_ids": jnp.searchsorted(jnp.cumsum(uneven(arg_keys[3], NBLK // 2, NBLK, 4, 1)), jnp.arange(NBLK), side="right").astype(jnp.int32),
        "half_order": draw_half_order(jax.random.fold_in(arg_keys[6], 71), 0),
        "out_weight": centred(arg_keys[5], (HEADS * HD, D), (HEADS * HD) ** -0.5, 0.125, ((0, 8),)),
    }


def attend_head(head_queries, head_keys, head_values, token_frame):
    block_rows = math.gcd(head_queries.shape[0], 512)
    query_blocks = head_queries.reshape(-1, block_rows, HD)
    frame_blocks = token_frame.reshape(-1, block_rows)

    def one_block(inputs):
        query_block, frame_block = inputs
        scores = jnp.dot(query_block, head_keys.T, preferred_element_type=jnp.float32) * (1.0 / math.sqrt(HD))
        scores = jnp.where(token_frame[None, :] <= frame_block[:, None], scores, -jnp.inf)
        top_score = lax.optimization_barrier(jnp.max(scores, axis=1, keepdims=True))
        weights = jnp.exp(scores - top_score)
        totals = lax.optimization_barrier(jnp.sum(weights, axis=1))
        numerator = jnp.dot(weights.astype(jnp.bfloat16), head_values, preferred_element_type=jnp.float32)
        return (numerator / totals[:, None]).astype(jnp.bfloat16)
    return lax.map(one_block, (query_blocks, frame_blocks)).reshape(-1, HD)

def by_head(matrix):
    return matrix.reshape(TOKENS, HEADS, HD).transpose(1, 0, 2)

def reference(queries, keys, values, frame_ids, half_order, out_weight):
    row_ids = jnp.arange(TOKENS, dtype=jnp.int32)
    half_rows = TOK_DEV // 2
    position = half_order[row_ids // half_rows] * half_rows + row_ids % half_rows
    token_frame = frame_ids[position // BLOCK]

    def one_head(inputs):
        return attend_head(inputs[0], inputs[1], inputs[2], token_frame)
    attended = lax.map(one_head, (by_head(queries), by_head(keys), by_head(values)))
    attended = attended.transpose(1, 0, 2).reshape(TOKENS, HEADS * HD)
    return jnp.dot(attended, out_weight, preferred_element_type=jnp.float32).astype(jnp.bfloat16)
```

```python
import functools
import math

import jax
import jax.numpy as jnp
from jax import lax
from jax.experimental import pallas as pl
from jax.experimental.pallas import tpu as pltpu
from jax.sharding import PartitionSpec as P

HD = 128
HALF = 256
ROWS = 512
NX, NY, NZ = 4, 4, 8
COLS = 512
SCALE = math.log2(math.e) / math.sqrt(HD)
HIDE = 2e30
LOWEST = -1e30
NT = (((1,), (1,)), ((), ()))
NN = (((1,), (0,)), ((), ()))


def kernel(
    order_ref, frames_ref, q_hbm, k_hbm, v_hbm, w_hbm, out_ref,
    q_buf, kv, acc, top, total, att, att_out, w_buf, out_acc,
    q_recv, kv_recv, att_recv, w_recv,
    first_send, ring_send, side_send, w_send, out_send, att_send, att_side_send,
):
    ctx, j = lax.axis_index("ctx"), lax.axis_index("head")
    z, x = ctx // NX, ctx % NX
    y, b = j // 2, j % 2
    slot, owner = x % 2, x // 2
    side = {"ctx": ctx, "head": y * 2 + 1 - b}
    up = {"ctx": ((z + 1) % NZ) * NX + x, "head": j}
    down = {"ctx": ((z + NZ - 1) % NZ) * NX + x, "head": j}
    y_up = {"ctx": ctx, "head": ((y + 1) % NY) * 2 + b}
    y_down = {"ctx": ctx, "head": ((y + NY - 1) % NY) * 2 + b}

    def across(i):
        return {"ctx": z * NX + 2 * b + i, "head": y * 2 + owner}

    def is_self(i):
        return jnp.logical_and(2 * b + i == x, owner == b)

    def remote(src, dst, send, recv, device):
        return pltpu.make_async_remote_copy(
            src_ref=src, dst_ref=dst, send_sem=send, recv_sem=recv,
            device_id=device, device_id_type=pl.DeviceIdType.MESH,
        )

    def arrived(ref, sem):
        pltpu.make_async_copy(ref, ref, sem).wait()

    def send_or_keep(i, src, dst, send, recv):
        @pl.when(is_self(i))
        def _():
            pltpu.make_async_copy(src, dst, recv).start()

        @pl.when(jnp.logical_not(is_self(i)))
        def _():
            remote(src, dst, send, recv, across(i)).start()

    def sent_across(i, src, dst, send, recv):
        @pl.when(jnp.logical_not(is_self(i)))
        def _():
            remote(src, dst, send, recv, across(i)).wait_send()

    barrier = pltpu.get_barrier_semaphore()
    for device in [{"ctx": ctx, "head": (j + d) % (2 * NY)} for d in range(1, 2 * NY)] + [up, down]:
        pl.semaphore_signal(barrier, inc=1, device_id=device, device_id_type=pl.DeviceIdType.MESH)
    for i in range(2):
        @pl.when(jnp.logical_not(is_self(i)))
        def _():
            pl.semaphore_signal(barrier, inc=1, device_id=across(i), device_id_type=pl.DeviceIdType.MESH)
    pl.semaphore_wait(barrier, 2 * NY - 1 + 2 + 2 - jnp.where(owner == b, 1, 0))

    def first_copies(i):
        cols = pl.ds(i * HD, HD)
        return (
            (k_hbm.at[:, cols], kv.at[slot, 0], first_send.at[i, 0], kv_recv.at[slot]),
            (v_hbm.at[:, cols], kv.at[slot, 1], first_send.at[i, 1], kv_recv.at[slot]),
            (q_hbm.at[:, cols], q_buf.at[slot], first_send.at[i, 2], q_recv.at[slot]),
        )

    for what in range(3):
        for i in range(2):
            send_or_keep(i, *first_copies(i)[what])

    def w_copy(n):
        ry, other = n % NY, n // NY
        target = ((y + ry) % NY) * 2 + (1 - b if other else b)
        place = (NY - ry) % NY + NY * other
        src = w_hbm.at[:, pl.ds(pl.multiple_of(target * COLS, COLS), COLS)]
        if n == 0:
            return pltpu.make_async_copy(src, w_buf.at[0], w_recv.at[0])
        return remote(src, w_buf.at[place], w_send.at[n], w_recv.at[place], {"ctx": ctx, "head": target})

    for n in range(2 * NY):
        w_copy(n).start()

    acc[...] = jnp.zeros_like(acc)
    total[...] = jnp.zeros_like(total)
    top[...] = jnp.full_like(top, LOWEST)

    def frame(c, h):
        return frames_ref[order_ref[2 * c + h]]

    q_frames = [frame(z * NX + 2 * b + n // 2, n % 2) for n in range(4)]

    def shards(g, core):
        s = 1 + (g - 1) // 2
        r = jnp.where(g == 0, 0, s)
        rc = (g + 1) % 2
        ends = jnp.logical_or(g == 0, g == 7)
        rc_a = jnp.where(ends, 0, rc)
        rc_b = jnp.where(ends, 1, rc)
        return (
            ((z + NZ - r) % NZ) * NX + 2 * core + rc_a,
            ((z + r) % NZ) * NX + 2 * core + rc_b,
        )

    def attend(first, g, core):
        c_a, c_b = shards(g, core)
        k_frames = [frame(c, h) for c in (c_a, c_b) for h in range(2)]
        keys = jnp.concatenate([kv[first, 0], kv[first + 1, 0]], axis=0)
        values = jnp.concatenate([kv[first, 1], kv[first + 1, 1]], axis=0)
        values = jnp.concatenate([values, jnp.ones_like(values)], axis=1)
        for t in range(4):
            rows = pl.ds(t * HALF, HALF)
            queries = q_buf[t // 2, pl.ds((t % 2) * HALF, HALF), :]
            scores = lax.dot_general(queries, keys, NT, preferred_element_type=jnp.float32)
            hide = [jnp.where(f <= q_frames[t], 0.0, HIDE) for f in k_frames]
            best = None
            for h in range(4):
                part = jnp.maximum(
                    scores[:, h * HALF : h * HALF + HD], scores[:, h * HALF + HD : (h + 1) * HALF]
                ) - hide[h]
                best = part if best is None else jnp.maximum(best, part)
            old = top[rows, :]
            new = jnp.maximum(old, jnp.max(best, axis=1, keepdims=True) * SCALE)
            weights = []
            for h in range(4):
                base = new + hide[h]
                for n in range(2):
                    col = h * HALF + n * HD
                    weights.append(jnp.exp2(scores[:, col : col + HD] * SCALE - base).astype(jnp.bfloat16))
            weights = jnp.concatenate(weights, axis=1)
            product = lax.dot_general(weights, values, NN, preferred_element_type=jnp.float32)
            shrink = jnp.exp2(old - new)
            acc[rows, :] = acc[rows, :] * shrink + product[:, :HD]
            total[rows, :] = total[rows, :] * shrink + product[:, HD:]
            top[rows, :] = new

    def ring_copy(e, later, sem, device):
        return remote(kv.at[e], kv.at[later], ring_send.at[sem], kv_recv.at[later], device)

    def side_copy(e):
        return remote(kv.at[e], kv.at[16 + e], side_send.at[e], kv_recv.at[16 + e], side)

    def first_ring(e, act):
        act(ring_copy(e, 2 + 2 * e, e, up))
        act(ring_copy(e, 3 + 2 * e, 16 + e, down))

    start = lambda copy: copy.start()
    sent = lambda copy: copy.wait_send()

    def step(g, carry):
        @pl.when(g == 0)
        def _():
            for e in range(2):
                arrived(kv.at[e], kv_recv.at[e])
                first_ring(e, start)
                side_copy(e).start()
            for n in range(2):
                arrived(q_buf.at[n], q_recv.at[n])

        @pl.when(jnp.logical_and(g >= 1, g <= 7))
        def _():
            a, c = 2 * g, 2 * g + 1
            arrived(kv.at[a], kv_recv.at[a])
            @pl.when(g <= 4)
            def _():
                ring_copy(a, a + 4, a, up).start()
            @pl.when(g == 5)
            def _():
                ring_copy(10, 14, 10, up).start()
            arrived(kv.at[c], kv_recv.at[c])
            @pl.when(g <= 4)
            def _():
                ring_copy(c, c + 4, c, down).start()
            @pl.when(g == 6)
            def _():
                ring_copy(13, 15, 13, down).start()
            side_copy(a).start()
            side_copy(c).start()

        @pl.when(g <= 7)
        def _():
            attend(2 * g, g, b)

        @pl.when(g >= 1)
        def _():
            n = 16 + 2 * (g - 1)
            arrived(kv.at[n], kv_recv.at[n])
            arrived(kv.at[n + 1], kv_recv.at[n + 1])
            attend(n, g - 1, 1 - b)

        return carry

    lax.fori_loop(0, 9, step, 0)

    def out_copy(i):
        return (att_out.at[i], att.at[0, 0, slot], out_send.at[i], att_recv.at[0, 0, slot])

    for i in range(2):
        rows = pl.ds(i * ROWS, ROWS)
        att_out[i] = (acc[rows, :] / total[rows, :]).astype(jnp.bfloat16)
        send_or_keep(i, *out_copy(i))

    def y_copy(ry, later, n, sem, device):
        return remote(att.at[0, ry, n], att.at[0, later, n], att_send.at[sem], att_recv.at[0, later, n], device)

    def att_side(ry, n):
        return remote(
            att.at[0, ry, n], att.at[1, ry, n], att_side_send.at[ry, n], att_recv.at[1, ry, n], side
        )

    y_copies = [
        y_copy(0, 3, 0, 0, y_up), y_copy(0, 1, 0, 1, y_down),
        y_copy(0, 3, 1, 2, y_up), y_copy(0, 1, 1, 3, y_down),
        y_copy(3, 2, 0, 4, y_up), y_copy(1, 2, 1, 5, y_down),
    ]

    def project(core, ry, first=False):
        place = ry + NY * core
        arrived(w_buf.at[place], w_recv.at[place])
        rows = jnp.concatenate([att[core, ry, 0], att[core, ry, 1]], axis=1)
        product = lax.dot_general(rows, w_buf[place], NN, preferred_element_type=jnp.float32)
        out_acc[...] = product if first else out_acc[...] + product

    for n in range(2):
        arrived(att.at[0, 0, n], att_recv.at[0, 0, n])
        y_copies[2 * n].start()
        y_copies[2 * n + 1].start()
        att_side(0, n).start()
    project(0, 0, True)
    for n in range(2):
        arrived(att.at[1, 0, n], att_recv.at[1, 0, n])
    project(1, 0)
    arrived(att.at[0, 3, 0], att_recv.at[0, 3, 0])
    y_copies[4].start()
    att_side(3, 0).start()
    arrived(att.at[0, 1, 0], att_recv.at[0, 1, 0])
    att_side(1, 0).start()
    arrived(att.at[0, 1, 1], att_recv.at[0, 1, 1])
    y_copies[5].start()
    att_side(1, 1).start()
    arrived(att.at[0, 3, 1], att_recv.at[0, 3, 1])
    att_side(3, 1).start()
    project(0, 3)
    project(0, 1)
    for ry in (3, 1):
        for n in range(2):
            arrived(att.at[1, ry, n], att_recv.at[1, ry, n])
        project(1, ry)
    for n in range(2):
        arrived(att.at[0, 2, n], att_recv.at[0, 2, n])
        att_side(2, n).start()
    project(0, 2)
    for n in range(2):
        arrived(att.at[1, 2, n], att_recv.at[1, 2, n])
    project(1, 2)
    out_ref[...] = out_acc[...].astype(out_ref.dtype)

    for i in range(2):
        for what in range(3):
            sent_across(i, *first_copies(i)[what])
        sent_across(i, *out_copy(i))
    for n in range(1, 2 * NY):
        w_copy(n).wait_send()
    for e in range(2):
        first_ring(e, sent)
    for e in range(2, 10):
        ring_copy(e, e + 4, e, up).wait_send()
    ring_copy(10, 14, 10, up).wait_send()
    ring_copy(13, 15, 13, down).wait_send()
    for e in range(16):
        side_copy(e).wait_send()
    for copy in y_copies:
        copy.wait_send()
    for ry in range(NY):
        for n in range(2):
            att_side(ry, n).wait_send()


def per_device(queries, keys, values, frame_ids, half_order, out_weight):
    any_space = pl.BlockSpec(memory_space=pl.ANY)
    smem = pl.BlockSpec(memory_space=pltpu.SMEM)
    bf16, f32 = jnp.bfloat16, jnp.float32
    dma = pltpu.SemaphoreType.DMA
    return pl.pallas_call(
        kernel,
        out_shape=jax.ShapeDtypeStruct((ROWS, COLS), bf16),
        in_specs=[smem, smem, any_space, any_space, any_space, any_space],
        out_specs=pl.BlockSpec(memory_space=pltpu.VMEM),
        scratch_shapes=[
            pltpu.VMEM((2, ROWS, HD), bf16),
            pltpu.VMEM((32, 2, ROWS, HD), bf16),
            pltpu.VMEM((2 * ROWS, HD), f32),
            pltpu.VMEM((2 * ROWS, HD), f32),
            pltpu.VMEM((2 * ROWS, HD), f32),
            pltpu.VMEM((2, NY, 2, ROWS, HD), bf16),
            pltpu.VMEM((2, ROWS, HD), bf16),
            pltpu.VMEM((2 * NY, 2 * HD, COLS), bf16),
            pltpu.VMEM((ROWS, COLS), f32),
            dma((2,)), dma((32,)), dma((2, NY, 2)), dma((2 * NY,)),
            dma((2, 3)), dma((18,)), dma((16,)), dma((2 * NY,)), dma((2,)), dma((6,)), dma((NY, 2)),
        ],
        compiler_params=pltpu.CompilerParams(
            collective_id=0, has_side_effects=True, vmem_limit_bytes=48 * 2**20
        ),
        name="attention_layer",
    )(half_order, frame_ids, queries, keys, values, out_weight)


def solution(mesh):
    placed = (P("ctx", "head"), P("ctx", "head"), P("ctx", "head"), P(), P(), P("head", None))
    return jax.shard_map(
        per_device, mesh=mesh, in_specs=placed, out_specs=P("ctx", "head"), check_vma=False
    )
```

```python
import math

import jax
import jax.numpy as jnp
from jax import lax
from jax.experimental import pallas as pl
from jax.experimental.pallas import tpu as pltpu
from jax.sharding import PartitionSpec as P

HD = 128
HALF = 256
ROWS = 512
NX, NY, NZ = 4, 4, 8
COLS = 512
SCALE = math.log2(math.e) / math.sqrt(HD)
HIDE = 2e30
LOWEST = -1e30
NT = (((1,), (1,)), ((), ()))
NN = (((1,), (0,)), ((), ()))


def kernel(
    order_ref, frames_ref, q_hbm, k_hbm, v_hbm, w_hbm, out_ref,
    q_buf, kv, acc, top, total, part_out, part_lse, part, lse, att, w_buf, out_acc,
    q_recv, kv_recv, part_recv, lse_recv, att_recv, w_recv,
    first_send, q_send, ring_send, side_send, w_send, part_send, lse_send, att_send, att_side_send,
):
    ctx, j = lax.axis_index("ctx"), lax.axis_index("head")
    z, x = ctx // NX, ctx % NX
    y, b = j // 2, j % 2
    k = z % 4

    def at(dz, core):
        return {"ctx": ((z + dz + 2 * NZ) % NZ) * NX + x, "head": y * 2 + core}

    side = at(0, 1 - b)
    x_up = {"ctx": z * NX + (x + 1) % NX, "head": j}
    x_down = {"ctx": z * NX + (x + NX - 1) % NX, "head": j}

    def remote(src, dst, send, recv, device):
        return pltpu.make_async_remote_copy(
            src_ref=src, dst_ref=dst, send_sem=send, recv_sem=recv,
            device_id=device, device_id_type=pl.DeviceIdType.MESH,
        )

    def arrived(ref, sem):
        pltpu.make_async_copy(ref, ref, sem).wait()

    def send_or_keep(keep, src, dst, send, recv, device):
        @pl.when(keep)
        def _():
            pltpu.make_async_copy(src, dst, recv).start()

        @pl.when(jnp.logical_not(keep))
        def _():
            remote(src, dst, send, recv, device).start()

    def sent_unless(keep, src, dst, send, recv, device):
        @pl.when(jnp.logical_not(keep))
        def _():
            remote(src, dst, send, recv, device).wait_send()

    def dist(i):
        return (z + NZ - 2 * b - i) % 4

    def kv_target(i):
        d = dist(i)
        two = jnp.where(z % 2 == 0, -2, 2)
        dz = jnp.where(d == 0, 0, jnp.where(d == 1, -1, jnp.where(d == 2, two, 1)))
        slot = jnp.where(d % 2 == 0, d // 2, (3 - d) // 2)
        return at(dz, d % 2), slot

    def own_head(i):
        return jnp.logical_and(dist(i) == 0, b == 0)

    barrier = pltpu.get_barrier_semaphore()

    def greet(device):
        pl.semaphore_signal(barrier, inc=1, device_id=device, device_id_type=pl.DeviceIdType.MESH)

    def greet_unless(keep, device):
        @pl.when(jnp.logical_not(keep))
        def _():
            greet(device)

    for device in [{"ctx": ctx, "head": (j + d) % (2 * NY)} for d in range(1, 2 * NY)] + [x_up, x_down]:
        greet(device)
    for i in range(2):
        greet_unless(own_head(i), at(-dist(i), dist(i) % 2))
        greet(at(-dist(i) - 4, dist(i) % 2))
    first_self = jnp.logical_and(b == 0, k < 2)
    for n in range(4):
        source = at(b + 2 * n, k // 2)
        same = at(b + 2 * n, b)
        if n == 0:
            greet_unless(first_self, source)
            greet_unless(b == 0, same)
        else:
            greet(source)
            greet(same)
    pl.semaphore_wait(
        barrier, 2 * NY - 1 + 2 + 12 - 2 * jnp.where(first_self, 1, 0) - jnp.where(b == 0, 1, 0)
    )

    def head_cols(i):
        return pl.ds(pl.multiple_of(i * HD, HD), HD)

    def kv_copy(i, what):
        device, slot = kv_target(i)
        src = (k_hbm, v_hbm)[what].at[:, head_cols(i)]
        return own_head(i), src, kv.at[slot, what], first_send.at[i, what], kv_recv.at[slot], device

    def q_copy(i, m):
        slot = dist(i) // 2 + 2 * m
        keep = jnp.logical_and(own_head(i), m == 0)
        device = at(-dist(i) - 4 * m, dist(i) % 2)
        return keep, q_hbm.at[:, head_cols(i)], q_buf.at[slot], q_send.at[i, m], q_recv.at[slot], device

    near_head = jnp.where(jnp.logical_or(dist(0) == 0, dist(0) == 3), 0, 1)
    heads = [near_head, 1 - near_head]
    nearer = [jnp.where(dist(i) < 2, 0, 1) for i in heads]
    for i in heads:
        for what in range(2):
            send_or_keep(*kv_copy(i, what))
    for i, m in zip(heads, nearer):
        send_or_keep(*q_copy(i, m))

    def w_copy(n):
        ry, other = n % NY, n // NY
        target = ((y + ry) % NY) * 2 + (1 - b if other else b)
        place = (NY - ry) % NY + NY * other
        src = w_hbm.at[:, pl.ds(pl.multiple_of(target * COLS, COLS), COLS)]
        if n == 0:
            return pltpu.make_async_copy(src, w_buf.at[0], w_recv.at[0])
        return remote(src, w_buf.at[place], w_send.at[n], w_recv.at[place], {"ctx": ctx, "head": target})

    acc[...] = jnp.zeros_like(acc)
    total[...] = jnp.zeros_like(total)
    top[...] = jnp.full_like(top, LOWEST)

    def ring_copy(e, later, sem, device):
        return remote(kv.at[e], kv.at[later], ring_send.at[sem], kv_recv.at[later], device)

    def side_copy(e):
        return remote(kv.at[e], kv.at[8 + e], side_send.at[e], kv_recv.at[8 + e], side)

    rings = [
        ring_copy(0, 2, 0, x_up), ring_copy(0, 3, 1, x_down),
        ring_copy(1, 4, 2, x_up), ring_copy(1, 5, 3, x_down),
        ring_copy(2, 6, 4, x_up), ring_copy(5, 7, 5, x_down),
    ]

    def take(e, forward=()):
        arrived(kv.at[e], kv_recv.at[e])
        for n in forward:
            rings[n].start()
        side_copy(e).start()

    take(0, (0, 1))
    take(1, (2, 3))
    for i, m in zip(heads, nearer):
        send_or_keep(*q_copy(i, 1 - m))
    for n in range(2 * NY):
        w_copy(n).start()

    def frame(c, h):
        return frames_ref[order_ref[2 * c + h]]

    def shard_of(core, rx, n):
        x_src = (x + rx) % NX
        even = jnp.where(n == 0, 0, jnp.where(z % 2 == 0, 2, -2))
        odd = jnp.where(n == 0, -1, 1)
        dz = jnp.where(core == 0, even, odd)
        return ((z + dz + NZ) % NZ) * NX + x_src

    def attend(tiles, g):
        q_frames = [frame(((z + b + 2 * (t // 2)) % NZ) * NX + x, t % 2) for t in tiles]
        rx_a = jnp.where(g == 0, 0, jnp.where(g == 3, 2, 3))
        rx_b = jnp.where(g == 0, 0, jnp.where(g == 3, 2, 1))
        n_a = jnp.where(g == 2, 1, 0)
        n_b = jnp.where(g == 1, 0, 1)

        def load(core):
            first = 8 * core + 2 * g
            keys = jnp.concatenate([kv[first, 0], kv[first + 1, 0]], axis=0)
            values = jnp.concatenate([kv[first, 1], kv[first + 1, 1]], axis=0)
            values = jnp.concatenate([values, jnp.ones_like(values)], axis=1)
            side_core = 1 - b if core else b
            shards = (shard_of(side_core, rx_a, n_a), shard_of(side_core, rx_b, n_b))
            return keys, values, [frame(c, h) for c in shards for h in range(2)]

        groups = [load(0), load(1)]

        def score(h, core):
            queries = q_buf[tiles[h] // 2, pl.ds(pl.multiple_of((tiles[h] % 2) * HALF, HALF), HALF), :]
            return lax.dot_general(queries, groups[core][0], NT, preferred_element_type=jnp.float32)

        def finish(h, core, scores):
            rows = pl.ds(pl.multiple_of(tiles[h] * HALF, HALF), HALF)
            hide = [jnp.where(f <= q_frames[h], 0.0, HIDE) for f in groups[core][2]]
            best = None
            for a in range(4):
                peak = jnp.maximum(
                    scores[:, a * HALF : a * HALF + HD], scores[:, a * HALF + HD : (a + 1) * HALF]
                ) - hide[a]
                best = peak if best is None else jnp.maximum(best, peak)
            old = top[rows, :]
            new = jnp.maximum(old, jnp.max(best, axis=1, keepdims=True) * SCALE)
            weights = []
            for a in range(4):
                floor = new + hide[a]
                for s in range(2):
                    col = a * HALF + s * HD
                    weights.append(jnp.exp2(scores[:, col : col + HD] * SCALE - floor).astype(jnp.bfloat16))
            weights = jnp.concatenate(weights, axis=1)
            product = lax.dot_general(weights, groups[core][1], NN, preferred_element_type=jnp.float32)
            shrink = jnp.exp2(old - new)
            acc[rows, :] = acc[rows, :] * shrink + product[:, :HD]
            total[rows, :] = total[rows, :] * shrink + product[:, HD:]
            top[rows, :] = new

        steps = [(0, 0), (1, 0), (0, 1), (1, 1)]
        scores = score(*steps[0])
        for s, here in enumerate(steps):
            following = score(*steps[s + 1]) if s < 3 else None
            finish(*here, scores)
            scores = following

    lanes = lax.broadcasted_iota(jnp.int32, (HD, HD), 1)
    diagonal = lanes == lax.broadcasted_iota(jnp.int32, (HD, HD), 0)

    def part_copies(t):
        device = at(b + 2 * (t // 2), b)
        quarter, m = t % 4, t // 4
        keep = jnp.logical_and(t < 2, b == 0)
        return (
            (keep, part_out.at[t], part.at[quarter, m], part_send.at[t], part_recv.at[quarter, m], device),
            (keep, part_lse.at[t], lse.at[quarter, m], lse_send.at[t], lse_recv.at[quarter, m], device),
        )

    def close(t):
        rows = pl.ds(pl.multiple_of(t * HALF, HALF), HALF)
        sums = jnp.maximum(total[rows, :], 0.5)
        part_out[t] = (acc[rows, :] / sums).astype(jnp.bfloat16)
        logs = top[rows, :] + jnp.log2(sums)
        for r in range(2):
            line = jnp.where(diagonal, logs[r * HD : (r + 1) * HD, :], 0.0)
            part_lse[t, r : r + 1, :] = jnp.sum(line, axis=0, keepdims=True)
        for copy in part_copies(t):
            send_or_keep(*copy)

    def y_copy(quarter, ry):
        device = {"ctx": ctx, "head": ((y + ry) % NY) * 2 + b}
        there = (NY - ry) % NY
        return remote(
            att.at[0, quarter, 0], att.at[0, quarter, there], att_send.at[quarter, ry - 1],
            att_recv.at[0, quarter, there], device,
        )

    def att_side(quarter, ry):
        return remote(
            att.at[0, quarter, ry], att.at[1, quarter, ry], att_side_send.at[quarter, ry],
            att_recv.at[1, quarter, ry], side,
        )

    def merge(quarter):
        for m in range(2):
            arrived(part.at[quarter, m], part_recv.at[quarter, m])
            arrived(lse.at[quarter, m], lse_recv.at[quarter, m])
        for r in range(2):
            rows = pl.ds(r * HD, HD)
            logs = []
            for m in range(2):
                line = jnp.broadcast_to(lse[quarter, m, r : r + 1, :], (HD, HD))
                logs.append(jnp.sum(jnp.where(diagonal, line, 0.0), axis=1, keepdims=True))
            high = jnp.maximum(logs[0], logs[1])
            shares = [jnp.exp2(log - high) for log in logs]
            whole = shares[0] + shares[1]
            mixed = sum(
                part[quarter, m, rows, :].astype(jnp.float32) * (shares[m] / whole) for m in range(2)
            )
            att[0, quarter, 0, rows, :] = mixed.astype(jnp.bfloat16)
        for ry in (1, 3, 2):
            y_copy(quarter, ry).start()
        att_side(quarter, 0).start()

    def step(i, carry):
        opening = i < 4
        n = jnp.where(i == 0, 0, jnp.where(i == 1, 3, i - 1))
        quarter = jnp.where(
            i < 8, i % 4, jnp.where(i < 10, i - 6, jnp.where(i < 14, (i - 10) // 2, i - 12))
        )
        g = jnp.where(
            i < 8, i // 4, jnp.where(i < 10, 2, jnp.where(i < 14, 2 + i % 2, 3))
        )
        tiles = (jnp.where(opening, 2 * n, quarter), jnp.where(opening, 2 * n + 1, quarter + 4))

        @pl.when(opening)
        def _():
            arrived(q_buf.at[n], q_recv.at[n])

        @pl.when(i == 0)
        def _():
            for e in range(8, 10):
                arrived(kv.at[e], kv_recv.at[e])

        @pl.when(i == 1)
        def _():
            take(2, (4,))
            take(3)

        @pl.when(i == 3)
        def _():
            take(4)
            take(5, (5,))

        @pl.when(i == 4)
        def _():
            for e in range(10, 12):
                arrived(kv.at[e], kv_recv.at[e])

        @pl.when(i == 8)
        def _():
            for e in range(12, 14):
                arrived(kv.at[e], kv_recv.at[e])

        @pl.when(i == 9)
        def _():
            for e in range(6, 8):
                take(e)

        @pl.when(i == 11)
        def _():
            for e in range(14, 16):
                arrived(kv.at[e], kv_recv.at[e])

        @pl.when(i == 14)
        def _():
            merge(0)

        attend(tiles, g)

        @pl.when(jnp.logical_or(i == 11, i >= 13))
        def _():
            close(tiles[0])
            close(tiles[1])

        return carry

    lax.fori_loop(0, 16, step, 0)

    def project(quarter):
        slot, h = quarter // 2, quarter % 2
        rows, weights = [], []
        for core in range(2):
            for ry in range(NY):
                t = 1 - b if core else b
                head = (z + NZ - t - 2 * slot) % 4
                place = ry + jnp.where(head // 2 == b, 0, NY)
                rows.append(att[core, quarter, ry])
                weights.append(w_buf[place, pl.ds(pl.multiple_of((head % 2) * HD, HD), HD), :])
        product = lax.dot_general(
            jnp.concatenate(rows, axis=1), jnp.concatenate(weights, axis=0), NN,
            preferred_element_type=jnp.float32,
        )
        here = pl.ds(h * HALF, HALF)
        if slot == 0:
            out_acc[here, :] = product
        else:
            out_ref[here, :] = (out_acc[here, :] + product).astype(out_ref.dtype)

    def gather(quarter):
        for ry in (1, 3, 2):
            arrived(att.at[0, quarter, ry], att_recv.at[0, quarter, ry])
            att_side(quarter, ry).start()

    def finish(quarter):
        for ry in range(NY):
            arrived(att.at[1, quarter, ry], att_recv.at[1, quarter, ry])
        project(quarter)

    merge(1)
    gather(0)
    merge(2)
    for n in range(2 * NY):
        arrived(w_buf.at[n], w_recv.at[n])
    finish(0)
    merge(3)
    for quarter in range(1, 4):
        gather(quarter)
        finish(quarter)

    for i in range(2):
        for what in range(2):
            sent_unless(*kv_copy(i, what))
            sent_unless(*q_copy(i, what))
    for n in range(1, 2 * NY):
        w_copy(n).wait_send()
    for copy in rings:
        copy.wait_send()
    for e in range(8):
        side_copy(e).wait_send()
    for t in range(8):
        for copy in part_copies(t):
            sent_unless(*copy)
    for quarter in range(4):
        for ry in range(1, NY):
            y_copy(quarter, ry).wait_send()
        for ry in range(NY):
            att_side(quarter, ry).wait_send()


def per_device(queries, keys, values, frame_ids, half_order, out_weight):
    hbm = pl.BlockSpec(memory_space=pltpu.HBM)
    smem = pl.BlockSpec(memory_space=pltpu.SMEM)
    bf16, f32 = jnp.bfloat16, jnp.float32
    dma = pltpu.SemaphoreType.DMA
    return pl.pallas_call(
        kernel,
        out_shape=jax.ShapeDtypeStruct((ROWS, COLS), bf16),
        in_specs=[smem, smem, hbm, hbm, hbm, hbm],
        out_specs=pl.BlockSpec(memory_space=pltpu.VMEM),
        scratch_shapes=[
            pltpu.VMEM((4, ROWS, HD), bf16),
            pltpu.VMEM((16, 2, ROWS, HD), bf16),
            pltpu.VMEM((4 * ROWS, HD), f32),
            pltpu.VMEM((4 * ROWS, HD), f32),
            pltpu.VMEM((4 * ROWS, HD), f32),
            pltpu.VMEM((8, HALF, HD), bf16),
            pltpu.VMEM((8, 8, HD), f32),
            pltpu.VMEM((4, 2, HALF, HD), bf16),
            pltpu.VMEM((4, 2, 8, HD), f32),
            pltpu.VMEM((2, 4, NY, HALF, HD), bf16),
            pltpu.VMEM((2 * NY, 2 * HD, COLS), bf16),
            pltpu.VMEM((ROWS, COLS), f32),
            dma((4,)), dma((16,)), dma((4, 2)), dma((4, 2)), dma((2, 4, NY)), dma((2 * NY,)),
            dma((2, 2)), dma((2, 2)), dma((6,)), dma((8,)), dma((2 * NY,)), dma((8,)), dma((8,)),
            dma((4, NY - 1)), dma((4, NY)),
        ],
        compiler_params=pltpu.CompilerParams(
            collective_id=0, has_side_effects=True, vmem_limit_bytes=62 * 2**20
        ),
        name="attention_layer",
    )(half_order, frame_ids, queries, keys, values, out_weight)


def solution(mesh):
    placed = (P("ctx", "head"), P("ctx", "head"), P("ctx", "head"), P(), P(), P("head", None))
    return jax.shard_map(
        per_device, mesh=mesh, in_specs=placed, out_specs=P("ctx", "head"), check_vma=False
    )
```

```python
import math

import jax
import jax.numpy as jnp
from jax import lax
from jax.experimental import pallas as pl
from jax.experimental.pallas import tpu as pltpu
from jax.sharding import PartitionSpec as P

HD = 128
HALF = 256
ROWS = 512
NX, NY, NZ = 4, 4, 8
COLS = 512
SCALE = math.log2(math.e) / math.sqrt(HD)
HIDE = 2e30
LOWEST = -1e30
LOG_ROWS = 16
NT = (((1,), (1,)), ((), ()))
NN = (((1,), (0,)), ((), ()))
SCHEDULE = [[(t, e + d) for t, d in ((0, 0), (1, 0), (1, 1), (6, 0), (7, 0), (7, 1))] for e in (0, 2, 4)] + [
    [(2, 0), (3, 0), (3, 1), (2, 2), (3, 2), (3, 3)],
    [(2, 4), (3, 4), (3, 5), (2, 6), (3, 6), (3, 7)],
    [(6, 6), (7, 6), (4, 0), (7, 7), (4, 2), (4, 4)],
    [(4, 6), (5, 0), (0, 6), (5, 1), (5, 2), (5, 3)],
    [(5, 4), (1, 6), (5, 5), (1, 7), (5, 6), (5, 7)],
]


def kernel(
    order_ref, frames_ref, q_hbm, k_hbm, v_hbm, w_hbm, out_ref,
    q_buf, kv, acc, top, total, part_out, part, att, w_buf, out_acc,
    key_frames, query_frames, beyond,
    q_recv, kv_recv, part_recv, att_recv, w_recv,
    first_send, q_send, ring_send, side_send, w_send, part_send, att_send, att_side_send,
):
    ctx, j = lax.axis_index("ctx"), lax.axis_index("head")
    z, x = ctx // NX, ctx % NX
    y, b = j // 2, j % 2
    k = z % 4

    def at(dz, core):
        return {"ctx": ((z + dz + 2 * NZ) % NZ) * NX + x, "head": y * 2 + core}

    side = at(0, 1 - b)
    x_up = {"ctx": z * NX + (x + 1) % NX, "head": j}
    x_down = {"ctx": z * NX + (x + NX - 1) % NX, "head": j}

    def remote(src, dst, send, recv, device):
        return pltpu.make_async_remote_copy(
            src_ref=src, dst_ref=dst, send_sem=send, recv_sem=recv,
            device_id=device, device_id_type=pl.DeviceIdType.MESH,
        )

    def arrived(ref, sem):
        pltpu.make_async_copy(ref, ref, sem).wait()

    def send_or_keep(keep, src, dst, send, recv, device):
        @pl.when(keep)
        def _():
            pltpu.make_async_copy(src, dst, recv).start()

        @pl.when(jnp.logical_not(keep))
        def _():
            remote(src, dst, send, recv, device).start()

    def sent_unless(keep, src, dst, send, recv, device):
        @pl.when(jnp.logical_not(keep))
        def _():
            remote(src, dst, send, recv, device).wait_send()

    def dist(i):
        return (z + NZ - 2 * b - i) % 4

    def kv_target(i):
        d = dist(i)
        two = jnp.where(z % 2 == 0, -2, 2)
        dz = jnp.where(d == 0, 0, jnp.where(d == 1, -1, jnp.where(d == 2, two, 1)))
        slot = jnp.where(d % 2 == 0, d // 2, (3 - d) // 2)
        return at(dz, d % 2), slot

    def own_head(i):
        return jnp.logical_and(dist(i) == 0, b == 0)

    barrier = pltpu.get_barrier_semaphore()

    def greet(device):
        pl.semaphore_signal(barrier, inc=1, device_id=device, device_id_type=pl.DeviceIdType.MESH)

    def greet_unless(keep, device):
        @pl.when(jnp.logical_not(keep))
        def _():
            greet(device)

    for device in [{"ctx": ctx, "head": (j + d) % (2 * NY)} for d in range(1, 2 * NY)] + [x_up, x_down]:
        greet(device)
    for i in range(2):
        greet_unless(own_head(i), at(-dist(i), dist(i) % 2))
        greet(at(-dist(i) - 4, dist(i) % 2))
    first_self = jnp.logical_and(b == 0, k < 2)
    for n in range(4):
        source = at(b + 2 * n, k // 2)
        same = at(b + 2 * n, b)
        if n == 0:
            greet_unless(first_self, source)
            greet_unless(b == 0, same)
        else:
            greet(source)
            greet(same)
    pl.semaphore_wait(
        barrier, 2 * NY - 1 + 2 + 12 - 2 * jnp.where(first_self, 1, 0) - jnp.where(b == 0, 1, 0)
    )

    def head_cols(i):
        return pl.ds(pl.multiple_of(i * HD, HD), HD)

    def kv_copy(i, what):
        device, slot = kv_target(i)
        src = (k_hbm, v_hbm)[what].at[:, head_cols(i)]
        return own_head(i), src, kv.at[slot, what], first_send.at[i, what], kv_recv.at[slot], device

    def q_copy(i, m):
        slot = dist(i) // 2 + 2 * m
        keep = jnp.logical_and(own_head(i), m == 0)
        device = at(-dist(i) - 4 * m, dist(i) % 2)
        return keep, q_hbm.at[:, head_cols(i)], q_buf.at[pl.ds(pl.multiple_of(slot * ROWS, ROWS), ROWS)], q_send.at[i, m], q_recv.at[slot], device

    near_head = jnp.where(jnp.logical_or(dist(0) == 0, dist(0) == 3), 0, 1)
    heads = [near_head, 1 - near_head]
    nearer = [jnp.where(dist(i) < 2, 0, 1) for i in heads]
    def near_queries(when):
        for i, m in zip(heads, nearer):
            @pl.when((dist(i) < 2) == when)
            def _():
                send_or_keep(*q_copy(i, m))

    near_queries(True)
    for i in heads:
        for what in range(2):
            send_or_keep(*kv_copy(i, what))
    near_queries(False)

    def w_copy(n):
        ry, other = n % NY, n // NY
        target = ((y + ry) % NY) * 2 + (1 - b if other else b)
        place = (NY - ry) % NY + NY * other
        src = w_hbm.at[:, pl.ds(pl.multiple_of(target * COLS, COLS), COLS)]
        if n == 0:
            return pltpu.make_async_copy(src, w_buf.at[0], w_recv.at[0])
        return remote(src, w_buf.at[place], w_send.at[n], w_recv.at[place], {"ctx": ctx, "head": target})

    acc[...] = jnp.zeros_like(acc)
    total[...] = jnp.zeros_like(total)
    top[...] = jnp.full_like(top, LOWEST)

    def ring_copy(e, later, sem, device):
        return remote(kv.at[e], kv.at[later], ring_send.at[sem], kv_recv.at[later], device)

    def side_copy(e):
        return remote(kv.at[e], kv.at[8 + e], side_send.at[e], kv_recv.at[8 + e], side)

    rings = [
        ring_copy(0, 2, 0, x_up), ring_copy(0, 3, 1, x_down),
        ring_copy(1, 4, 2, x_up), ring_copy(1, 5, 3, x_down),
        ring_copy(2, 6, 4, x_up), ring_copy(5, 7, 5, x_down),
    ]

    def take(e, forward=()):
        arrived(kv.at[e], kv_recv.at[e])
        for n in forward:
            rings[n].start()
        side_copy(e).start()

    take(0, (0, 1))

    @pl.when(b == 0)
    def _():
        take(2, (4,))

    @pl.when(b == 1)
    def _():
        take(1, (2, 3))

    def far_queries(when):
        for i, m in zip(heads, nearer):
            @pl.when((dist(i) >= 2) == when)
            def _():
                remote(*q_copy(i, 1 - m)[1:]).start()

    far_queries(True)

    for n in range(2 * NY):
        w_copy(n).start()

    def frame(c, h):
        return frames_ref[order_ref[2 * c + h]]

    def shard_of(core, rx, n):
        x_src = (x + rx) % NX
        even = jnp.where(n == 0, 0, jnp.where(z % 2 == 0, 2, -2))
        odd = jnp.where(n == 0, -1, 1)
        dz = jnp.where(core == 0, even, odd)
        return ((z + dz + NZ) % NZ) * NX + x_src

    def shard_of_piece(core, e):
        rx = 0 if e < 2 else 2 if e >= 6 else 3 - 2 * (e % 2)
        return shard_of(core, rx, e if e < 2 else e - 6 if e >= 6 else (e - 2) // 2)

    middle = order_ref.shape[0] // 2
    places, founds = [0, 0, 0], [0, 0, 0]
    for e in range(8):
        for core in range(2):
            c = shard_of_piece(1 - b if core else b, e)
            for h in range(2):
                key_frames[2 * (8 * core + e) + h] = frame(c, h)
            upper = order_ref[2 * c + 1]
            for p in range(3):
                here = jnp.where(upper == middle + p, 1, 0)
                places[p] += here * (8 * core + e)
                founds[p] += here
    for p in range(3):
        beyond[p] = places[p]
        beyond[3 + p] = founds[p]
    for n in range(4):
        for h in range(2):
            query_frames[2 * n + h] = frame(((z + b + 2 * n) % NZ) * NX + x, h)

    def meet(steps):
        def score(t, load, hide):
            queries = q_buf[pl.ds(pl.multiple_of(t * HALF, HALF), HALF), :]
            return lax.dot_general(queries, load(0), NT, preferred_element_type=jnp.float32)

        def finish(t, load, hide, scores):
            values = load(1)
            values = jnp.concatenate([values, jnp.ones_like(values)], axis=1)
            rows = pl.ds(pl.multiple_of(t * HALF, HALF), HALF)
            hide = [jnp.where(hidden, HIDE, 0.0) for hidden in hide]
            best = None
            for a in range(len(hide)):
                peak = jnp.maximum(
                    scores[:, a * HALF : a * HALF + HD], scores[:, a * HALF + HD : (a + 1) * HALF]
                ) - hide[a]
                best = peak if best is None else jnp.maximum(best, peak)
            old = top[rows, :]
            new = jnp.maximum(old, jnp.max(best, axis=1, keepdims=True) * SCALE)
            weights = []
            for a in range(len(hide)):
                floor = new + hide[a]
                for half in range(2):
                    col = a * HALF + half * HD
                    weights.append(jnp.exp2(scores[:, col : col + HD] * SCALE - floor).astype(jnp.bfloat16))
            weights = jnp.concatenate(weights, axis=1)
            product = lax.dot_general(weights, values, NN, preferred_element_type=jnp.float32)
            shrink = jnp.exp2(old - new)
            acc[rows, :] = acc[rows, :] * shrink + product[:, :HD]
            total[rows, :] = total[rows, :] * shrink + product[:, HD:]
            top[rows, :] = new

        scores = score(*steps[0])
        for s, here in enumerate(steps):
            following = score(*steps[s + 1]) if s + 1 < len(steps) else None
            finish(*here, scores)
            scores = following

    def keys_step(t, e, low):
        blocks = []
        for a in range(4):
            piece = jnp.where(low == 1, 8 * (a % 2) + a // 2 + e, 8 * (a // 2) + e)
            blocks.append((piece, (1 - low) * (a % 2)))

        def load(what):
            return jnp.concatenate(
                [
                    kv[piece, what, pl.ds(pl.multiple_of(half * HALF, HALF), HALF), :]
                    for piece, half in blocks
                ],
                axis=0,
            )

        q_frame = query_frames[t]
        return t, load, [key_frames[2 * piece + half] > q_frame for piece, half in blocks]

    def across_middle(tiles):
        def load(what):
            return jnp.concatenate([kv[beyond[p], what, pl.ds(HALF, HALF), :] for p in range(3)], axis=0)

        steps = []
        for t in tiles:
            low = query_frames[t]
            hide = [
                jnp.logical_or(beyond[3 + p] == 0, frames_ref[middle + p] > low) for p in range(3)
            ]
            steps.append((t, load, hide))
        meet(steps)

    lanes = lax.broadcasted_iota(jnp.int32, (HD, HD), 1)
    log_row = lax.broadcasted_iota(jnp.int32, (LOG_ROWS, HD), 0)
    diagonal = lanes == lax.broadcasted_iota(jnp.int32, (HD, HD), 0)

    def part_copy(t):
        device = at(b + 2 * (t // 2), b)
        quarter, m = t % 4, t // 4
        keep = jnp.logical_and(t < 2, b == 0)
        return keep, part_out.at[t], part.at[quarter, m], part_send.at[t], part_recv.at[quarter, m], device

    def close(t):
        rows = pl.ds(pl.multiple_of(t * HALF, HALF), HALF)
        sums = jnp.maximum(total[rows, :], 0.5)
        part_out[t, pl.ds(0, HALF), :] = (acc[rows, :] / sums).astype(jnp.bfloat16)
        logs = top[rows, :] + jnp.log2(sums)
        tail = jnp.zeros((LOG_ROWS, HD), jnp.float32)
        for r in range(2):
            line = jnp.where(diagonal, logs[r * HD : (r + 1) * HD, :], 0.0)
            rest = jnp.sum(line, axis=0, keepdims=True)
            for term in range(3):
                rounded = rest.astype(jnp.bfloat16).astype(jnp.float32)
                tail = jnp.where(log_row == 2 * term + r, rounded, tail)
                rest = rest - rounded
        part_out[t, pl.ds(HALF, LOG_ROWS), :] = tail.astype(jnp.bfloat16)
        send_or_keep(*part_copy(t))

    def y_copy(quarter, ry):
        device = {"ctx": ctx, "head": ((y + ry) % NY) * 2 + b}
        there = (NY - ry) % NY
        return remote(
            att.at[0, quarter, 0], att.at[0, quarter, there], att_send.at[quarter, ry - 1],
            att_recv.at[0, quarter, there], device,
        )

    def att_side(quarter, ry):
        return remote(
            att.at[0, quarter, ry], att.at[1, quarter, ry], att_side_send.at[quarter, ry],
            att_recv.at[1, quarter, ry], side,
        )

    def merge(quarter):
        for m in range(2):
            arrived(part.at[quarter, m], part_recv.at[quarter, m])
        tails = [part[quarter, m, pl.ds(HALF, LOG_ROWS), :].astype(jnp.float32) for m in range(2)]
        for r in range(2):
            rows = pl.ds(r * HD, HD)
            logs = []
            for m in range(2):
                line = sum(tails[m][2 * term + r : 2 * term + r + 1, :] for term in range(3))
                line = jnp.broadcast_to(line, (HD, HD))
                logs.append(jnp.sum(jnp.where(diagonal, line, 0.0), axis=1, keepdims=True))
            high = jnp.maximum(logs[0], logs[1])
            shares = [jnp.exp2(log - high) for log in logs]
            whole = shares[0] + shares[1]
            mixed = sum(
                part[quarter, m, rows, :].astype(jnp.float32) * (shares[m] / whole) for m in range(2)
            )
            att[0, quarter, 0, rows, :] = mixed.astype(jnp.bfloat16)
        for ry in (1, 3, 2):
            y_copy(quarter, ry).start()
        att_side(quarter, 0).start()

    def from_side(*pieces):
        for e in pieces:
            arrived(kv.at[8 + e], kv_recv.at[8 + e])

    def step(i, carry):
        def now(key):
            return sum(jnp.where(i == item, entry, 0) for item, entry in enumerate(key) if entry)

        def event(when, act, *args):
            @pl.when(when)
            def _():
                act(*args)

        first_core, second_core = b == 0, b == 1
        event(jnp.logical_and(i == 0, first_core), take, 1, (2, 3))
        event(i == 0, lambda: [arrived(q_buf.at[pl.ds(n * ROWS, ROWS)], q_recv.at[n]) for n in (0, 3)])
        event(i == 0, far_queries, False)
        event(jnp.logical_and(i == 0, second_core), take, 2, (4,))
        event(i == 0, take, 3)
        event(i == 0, from_side, 0, 1)
        event(i == 1, take, 5, (5,))
        event(i == 1, take, 4)
        event(i == 1, from_side, 2, 3)
        event(i == 2, take, 6)
        event(i == 2, from_side, 4, 5)
        event(i == 3, lambda: arrived(q_buf.at[pl.ds(ROWS, ROWS)], q_recv.at[1]))
        event(i == 3, take, 7)
        event(i == 4, from_side, 6, 7)
        event(i == 5, lambda: arrived(q_buf.at[pl.ds(2 * ROWS, ROWS)], q_recv.at[2]))

        event(i == 7, merge, 2)
        event(i == 7, merge, 3)

        meet(
            [
                keys_step(
                    now([item[s][0] for item in SCHEDULE]),
                    now([item[s][1] for item in SCHEDULE]),
                    now([1 - item[s][0] % 2 for item in SCHEDULE]),
                )
                for s in range(6)
            ]
        )

        event(i == 4, lambda: across_middle([2]))
        event(i == 5, lambda: across_middle([6]))
        event(i == 6, lambda: across_middle([4, 0]))

        @pl.when(i >= 4)
        def _():
            close(now((0, 0, 0, 0, 2, 6, 4, 5)))
            close(now((0, 0, 0, 0, 3, 7, 0, 1)))

        return carry

    lax.fori_loop(0, 8, step, 0)

    def project(quarter):
        slot, h = quarter // 2, quarter % 2
        rows, weights = [], []
        for core in range(2):
            for ry in range(NY):
                t = 1 - b if core else b
                head = (z + NZ - t - 2 * slot) % 4
                place = ry + jnp.where(head // 2 == b, 0, NY)
                rows.append(att[core, quarter, ry])
                weights.append(w_buf[place, pl.ds(pl.multiple_of((head % 2) * HD, HD), HD), :])
        product = lax.dot_general(
            jnp.concatenate(rows, axis=1), jnp.concatenate(weights, axis=0), NN,
            preferred_element_type=jnp.float32,
        )
        here = pl.ds(h * HALF, HALF)
        if slot == 1:
            out_acc[here, :] = product
        else:
            out_ref[here, :] = (out_acc[here, :] + product).astype(out_ref.dtype)

    def gather(quarter):
        for ry in (1, 3, 2):
            arrived(att.at[0, quarter, ry], att_recv.at[0, quarter, ry])
            att_side(quarter, ry).start()

    def finish(quarter):
        for ry in range(NY):
            arrived(att.at[1, quarter, ry], att_recv.at[1, quarter, ry])
        project(quarter)

    for i in range(2):
        for what in range(2):
            sent_unless(*kv_copy(i, what))
            sent_unless(*q_copy(i, what))
    for n in range(1, 2 * NY):
        w_copy(n).wait_send()
    for copy in rings:
        copy.wait_send()
    for e in range(8):
        side_copy(e).wait_send()
    for n in range(2 * NY):
        arrived(w_buf.at[n], w_recv.at[n])
    merge(0)
    gather(2)
    gather(3)
    finish(2)
    merge(1)
    finish(3)
    gather(0)
    gather(1)
    finish(0)
    finish(1)
    for t in range(8):
        sent_unless(*part_copy(t))
    for quarter in range(4):
        for ry in range(1, NY):
            y_copy(quarter, ry).wait_send()
        for ry in range(NY):
            att_side(quarter, ry).wait_send()


def per_device(queries, keys, values, frame_ids, half_order, out_weight):
    hbm = pl.BlockSpec(memory_space=pltpu.HBM)
    smem = pl.BlockSpec(memory_space=pltpu.SMEM)
    bf16, f32 = jnp.bfloat16, jnp.float32
    dma = pltpu.SemaphoreType.DMA
    return pl.pallas_call(
        kernel,
        out_shape=jax.ShapeDtypeStruct((ROWS, COLS), bf16),
        in_specs=[smem, smem, hbm, hbm, hbm, hbm],
        out_specs=pl.BlockSpec(memory_space=pltpu.VMEM),
        scratch_shapes=[
            pltpu.VMEM((4 * ROWS, HD), bf16),
            pltpu.VMEM((16, 2, ROWS, HD), bf16),
            pltpu.VMEM((4 * ROWS, HD), f32),
            pltpu.VMEM((4 * ROWS, HD), f32),
            pltpu.VMEM((4 * ROWS, HD), f32),
            pltpu.VMEM((8, HALF + LOG_ROWS, HD), bf16),
            pltpu.VMEM((4, 2, HALF + LOG_ROWS, HD), bf16),
            pltpu.VMEM((2, 4, NY, HALF, HD), bf16),
            pltpu.VMEM((2 * NY, 2 * HD, COLS), bf16),
            pltpu.VMEM((ROWS, COLS), f32),
            pltpu.SMEM((32,), jnp.int32),
            pltpu.SMEM((8,), jnp.int32),
            pltpu.SMEM((6,), jnp.int32),
            dma((4,)), dma((16,)), dma((4, 2)), dma((2, 4, NY)), dma((2 * NY,)),
            dma((2, 2)), dma((2, 2)), dma((6,)), dma((8,)), dma((2 * NY,)), dma((8,)),
            dma((4, NY - 1)), dma((4, NY)),
        ],
        compiler_params=pltpu.CompilerParams(
            collective_id=0, has_side_effects=True, vmem_limit_bytes=62 * 2**20
        ),
        name="attention_layer",
    )(half_order, frame_ids, queries, keys, values, out_weight)


def solution(mesh):
    placed = (P("ctx", "head"), P("ctx", "head"), P("ctx", "head"), P(), P(), P("head", None))
    return jax.shard_map(
        per_device, mesh=mesh, in_specs=placed, out_specs=P("ctx", "head"), check_vma=False
    )
```

```python
import math

import jax
import jax.numpy as jnp
from jax import lax
from jax.experimental import pallas as pl
from jax.experimental.pallas import tpu as pltpu
from jax.sharding import PartitionSpec as P

HD = 128
HALF = 256
ROWS = 512
NX, NY, NZ = 4, 4, 8
COLS = 512
SCALE = math.log2(math.e) / math.sqrt(HD)
HIDE = 2e30
LOWEST = -1e30
LOG_ROWS = 16
NT = (((1,), (1,)), ((), ()))
NN = (((1,), (0,)), ((), ()))
SCHEDULE = [[(t, e + d) for t, d in ((0, 0), (1, 0), (1, 1), (6, 0), (7, 0), (7, 1))] for e in (0, 2, 4)] + [
    [(2, 0), (3, 0), (3, 1), (2, 2), (3, 2), (3, 3)],
    [(2, 4), (3, 4), (3, 5), (2, 6), (3, 6), (3, 7)],
    [(6, 6), (7, 6), (4, 0), (7, 7), (4, 2), (4, 4)],
    [(4, 6), (5, 0), (0, 6), (5, 1), (5, 2), (5, 3)],
    [(5, 4), (1, 6), (5, 5), (1, 7), (5, 6), (5, 7)],
]


def kernel(
    order_ref, frames_ref, q_hbm, k_hbm, v_hbm, w_hbm, out_ref,
    q_buf, kv, acc, top, total, part_out, part, att, w_buf, out_acc,
    key_frames, query_frames, beyond,
    q_recv, kv_recv, part_recv, att_recv, w_recv,
    first_send, q_send, ring_send, side_send, w_send, part_send, att_send, att_side_send,
):
    ctx, j = lax.axis_index("ctx"), lax.axis_index("head")
    z, x = ctx // NX, ctx % NX
    y, b = j // 2, j % 2
    k = z % 4

    def at(dz, core):
        return {"ctx": ((z + dz + 2 * NZ) % NZ) * NX + x, "head": y * 2 + core}

    side = at(0, 1 - b)
    x_up = {"ctx": z * NX + (x + 1) % NX, "head": j}
    x_down = {"ctx": z * NX + (x + NX - 1) % NX, "head": j}

    def remote(src, dst, send, recv, device):
        return pltpu.make_async_remote_copy(
            src_ref=src, dst_ref=dst, send_sem=send, recv_sem=recv,
            device_id=device, device_id_type=pl.DeviceIdType.MESH,
        )

    def arrived(ref, sem):
        pltpu.make_async_copy(ref, ref, sem).wait()

    def send_or_keep(keep, src, dst, send, recv, device):
        @pl.when(keep)
        def _():
            pltpu.make_async_copy(src, dst, recv).start()

        @pl.when(jnp.logical_not(keep))
        def _():
            remote(src, dst, send, recv, device).start()

    def sent_unless(keep, src, dst, send, recv, device):
        @pl.when(jnp.logical_not(keep))
        def _():
            remote(src, dst, send, recv, device).wait_send()

    def dist(i):
        return (z + NZ - 2 * b - i) % 4

    def kv_target(i):
        d = dist(i)
        two = jnp.where(z % 2 == 0, -2, 2)
        dz = jnp.where(d == 0, 0, jnp.where(d == 1, -1, jnp.where(d == 2, two, 1)))
        slot = jnp.where(d % 2 == 0, d // 2, (3 - d) // 2)
        return at(dz, d % 2), slot

    def own_head(i):
        return jnp.logical_and(dist(i) == 0, b == 0)

    barrier = pltpu.get_barrier_semaphore()

    def greet(device):
        pl.semaphore_signal(barrier, inc=1, device_id=device, device_id_type=pl.DeviceIdType.MESH)

    def greet_unless(keep, device):
        @pl.when(jnp.logical_not(keep))
        def _():
            greet(device)

    for device in [{"ctx": ctx, "head": (j + d) % (2 * NY)} for d in range(1, 2 * NY)] + [x_up, x_down]:
        greet(device)
    for i in range(2):
        greet_unless(own_head(i), at(-dist(i), dist(i) % 2))
        greet(at(-dist(i) - 4, dist(i) % 2))
    first_self = jnp.logical_and(b == 0, k < 2)
    for n in range(4):
        source = at(b + 2 * n, k // 2)
        same = at(b + 2 * n, b)
        if n == 0:
            greet_unless(first_self, source)
            greet_unless(b == 0, same)
        else:
            greet(source)
            greet(same)
    pl.semaphore_wait(
        barrier, 2 * NY - 1 + 2 + 12 - 2 * jnp.where(first_self, 1, 0) - jnp.where(b == 0, 1, 0)
    )

    def head_cols(i):
        return pl.ds(pl.multiple_of(i * HD, HD), HD)

    def kv_copy(i, what):
        device, slot = kv_target(i)
        src = (k_hbm, v_hbm)[what].at[:, head_cols(i)]
        return own_head(i), src, kv.at[slot, what], first_send.at[i, what], kv_recv.at[slot], device

    def q_copy(i, m):
        slot = dist(i) // 2 + 2 * m
        keep = jnp.logical_and(own_head(i), m == 0)
        device = at(-dist(i) - 4 * m, dist(i) % 2)
        return keep, q_hbm.at[:, head_cols(i)], q_buf.at[pl.ds(pl.multiple_of(slot * ROWS, ROWS), ROWS)], q_send.at[i, m], q_recv.at[slot], device

    near_head = jnp.where(jnp.logical_or(dist(0) == 0, dist(0) == 3), 0, 1)
    heads = [near_head, 1 - near_head]
    nearer = [jnp.where(dist(i) < 2, 0, 1) for i in heads]
    def near_queries(when):
        for i, m in zip(heads, nearer):
            @pl.when((dist(i) < 2) == when)
            def _():
                send_or_keep(*q_copy(i, m))

    for i in heads:
        for what in range(2):
            send_or_keep(*kv_copy(i, what))
    near_queries(True)
    near_queries(False)

    def w_copy(n):
        ry, other = n % NY, n // NY
        target = ((y + ry) % NY) * 2 + (1 - b if other else b)
        place = (NY - ry) % NY + NY * other
        src = w_hbm.at[:, pl.ds(pl.multiple_of(target * COLS, COLS), COLS)]
        if n == 0:
            return pltpu.make_async_copy(src, w_buf.at[0], w_recv.at[0])
        return remote(src, w_buf.at[place], w_send.at[n], w_recv.at[place], {"ctx": ctx, "head": target})

    acc[...] = jnp.zeros_like(acc)
    total[...] = jnp.zeros_like(total)
    top[...] = jnp.full_like(top, LOWEST)

    def ring_copy(e, later, sem, device):
        return remote(kv.at[e], kv.at[later], ring_send.at[sem], kv_recv.at[later], device)

    def side_copy(e):
        return remote(kv.at[e], kv.at[8 + e], side_send.at[e], kv_recv.at[8 + e], side)

    rings = [
        ring_copy(0, 2, 0, x_up), ring_copy(0, 3, 1, x_down),
        ring_copy(1, 4, 2, x_up), ring_copy(1, 5, 3, x_down),
        ring_copy(2, 6, 4, x_up), ring_copy(5, 7, 5, x_down),
    ]

    def take(e, forward=()):
        arrived(kv.at[e], kv_recv.at[e])
        for n in forward:
            rings[n].start()
        side_copy(e).start()

    take(0, (0, 1))

    @pl.when(b == 0)
    def _():
        take(2, (4,))

    @pl.when(b == 1)
    def _():
        take(1, (2, 3))

    def far_queries(when):
        for i, m in zip(heads, nearer):
            @pl.when((dist(i) >= 2) == when)
            def _():
                remote(*q_copy(i, 1 - m)[1:]).start()

    far_queries(True)

    for n in range(2 * NY):
        w_copy(n).start()

    def frame(c, h):
        return frames_ref[order_ref[2 * c + h]]

    def shard_of(core, rx, n):
        x_src = (x + rx) % NX
        even = jnp.where(n == 0, 0, jnp.where(z % 2 == 0, 2, -2))
        odd = jnp.where(n == 0, -1, 1)
        dz = jnp.where(core == 0, even, odd)
        return ((z + dz + NZ) % NZ) * NX + x_src

    def shard_of_piece(core, e):
        rx = 0 if e < 2 else 2 if e >= 6 else 3 - 2 * (e % 2)
        return shard_of(core, rx, e if e < 2 else e - 6 if e >= 6 else (e - 2) // 2)

    middle = order_ref.shape[0] // 2
    places, founds = [0, 0, 0], [0, 0, 0]
    for e in range(8):
        for core in range(2):
            c = shard_of_piece(1 - b if core else b, e)
            for h in range(2):
                key_frames[2 * (8 * core + e) + h] = frame(c, h)
            upper = order_ref[2 * c + 1]
            for p in range(3):
                here = jnp.where(upper == middle + p, 1, 0)
                places[p] += here * (8 * core + e)
                founds[p] += here
    for p in range(3):
        beyond[p] = places[p]
        beyond[3 + p] = founds[p]
    for n in range(4):
        for h in range(2):
            query_frames[2 * n + h] = frame(((z + b + 2 * n) % NZ) * NX + x, h)

    def meet(steps):
        def score(t, load, hide):
            queries = q_buf[pl.ds(pl.multiple_of(t * HALF, HALF), HALF), :]
            return lax.dot_general(queries, load(0), NT, preferred_element_type=jnp.float32)

        def finish(t, load, hide, scores):
            values = load(1)
            values = jnp.concatenate([values, jnp.ones_like(values)], axis=1)
            rows = pl.ds(pl.multiple_of(t * HALF, HALF), HALF)
            hide = [jnp.where(hidden, HIDE, 0.0) for hidden in hide]
            best = None
            for a in range(len(hide)):
                peak = jnp.maximum(
                    scores[:, a * HALF : a * HALF + HD], scores[:, a * HALF + HD : (a + 1) * HALF]
                ) - hide[a]
                best = peak if best is None else jnp.maximum(best, peak)
            old = top[rows, :]
            new = jnp.maximum(old, jnp.max(best, axis=1, keepdims=True) * SCALE)
            weights = []
            for a in range(len(hide)):
                floor = new + hide[a]
                for half in range(2):
                    col = a * HALF + half * HD
                    weights.append(jnp.exp2(scores[:, col : col + HD] * SCALE - floor).astype(jnp.bfloat16))
            weights = jnp.concatenate(weights, axis=1)
            product = lax.dot_general(weights, values, NN, preferred_element_type=jnp.float32)
            shrink = jnp.exp2(old - new)
            acc[rows, :] = acc[rows, :] * shrink + product[:, :HD]
            total[rows, :] = total[rows, :] * shrink + product[:, HD:]
            top[rows, :] = new

        scores = score(*steps[0])
        for s, here in enumerate(steps):
            following = score(*steps[s + 1]) if s + 1 < len(steps) else None
            finish(*here, scores)
            scores = following

    def keys_step(t, e, low):
        blocks = []
        for a in range(4):
            piece = jnp.where(low == 1, 8 * (a % 2) + a // 2 + e, 8 * (a // 2) + e)
            blocks.append((piece, (1 - low) * (a % 2)))

        def load(what):
            return jnp.concatenate(
                [
                    kv[piece, what, pl.ds(pl.multiple_of(half * HALF, HALF), HALF), :]
                    for piece, half in blocks
                ],
                axis=0,
            )

        q_frame = query_frames[t]
        return t, load, [key_frames[2 * piece + half] > q_frame for piece, half in blocks]

    def across_middle(tiles):
        def load(what):
            return jnp.concatenate([kv[beyond[p], what, pl.ds(HALF, HALF), :] for p in range(3)], axis=0)

        steps = []
        for t in tiles:
            low = query_frames[t]
            hide = [
                jnp.logical_or(beyond[3 + p] == 0, frames_ref[middle + p] > low) for p in range(3)
            ]
            steps.append((t, load, hide))
        meet(steps)

    lanes = lax.broadcasted_iota(jnp.int32, (HD, HD), 1)
    log_row = lax.broadcasted_iota(jnp.int32, (LOG_ROWS, HD), 0)
    diagonal = lanes == lax.broadcasted_iota(jnp.int32, (HD, HD), 0)

    def part_copy(t):
        device = at(b + 2 * (t // 2), b)
        quarter, m = t % 4, t // 4
        keep = jnp.logical_and(t < 2, b == 0)
        return keep, part_out.at[t], part.at[quarter, m], part_send.at[t], part_recv.at[quarter, m], device

    def close(t):
        rows = pl.ds(pl.multiple_of(t * HALF, HALF), HALF)
        sums = jnp.maximum(total[rows, :], 0.5)
        part_out[t, pl.ds(0, HALF), :] = (acc[rows, :] / sums).astype(jnp.bfloat16)
        logs = top[rows, :] + jnp.log2(sums)
        tail = jnp.zeros((LOG_ROWS, HD), jnp.float32)
        for r in range(2):
            line = jnp.where(diagonal, logs[r * HD : (r + 1) * HD, :], 0.0)
            rest = jnp.sum(line, axis=0, keepdims=True)
            for term in range(3):
                rounded = rest.astype(jnp.bfloat16).astype(jnp.float32)
                tail = jnp.where(log_row == 2 * term + r, rounded, tail)
                rest = rest - rounded
        part_out[t, pl.ds(HALF, LOG_ROWS), :] = tail.astype(jnp.bfloat16)
        send_or_keep(*part_copy(t))

    def y_copy(quarter, ry):
        device = {"ctx": ctx, "head": ((y + ry) % NY) * 2 + b}
        there = (NY - ry) % NY
        return remote(
            att.at[0, quarter, 0], att.at[0, quarter, there], att_send.at[quarter, ry - 1],
            att_recv.at[0, quarter, there], device,
        )

    def att_side(quarter, ry):
        return remote(
            att.at[0, quarter, ry], att.at[1, quarter, ry], att_side_send.at[quarter, ry],
            att_recv.at[1, quarter, ry], side,
        )

    def merge(quarter):
        for m in range(2):
            arrived(part.at[quarter, m], part_recv.at[quarter, m])
        tails = [part[quarter, m, pl.ds(HALF, LOG_ROWS), :].astype(jnp.float32) for m in range(2)]
        for r in range(2):
            rows = pl.ds(r * HD, HD)
            logs = []
            for m in range(2):
                line = sum(tails[m][2 * term + r : 2 * term + r + 1, :] for term in range(3))
                line = jnp.broadcast_to(line, (HD, HD))
                logs.append(jnp.sum(jnp.where(diagonal, line, 0.0), axis=1, keepdims=True))
            high = jnp.maximum(logs[0], logs[1])
            shares = [jnp.exp2(log - high) for log in logs]
            whole = shares[0] + shares[1]
            mixed = sum(
                part[quarter, m, rows, :].astype(jnp.float32) * (shares[m] / whole) for m in range(2)
            )
            att[0, quarter, 0, rows, :] = mixed.astype(jnp.bfloat16)
        for ry in (1, 3, 2):
            y_copy(quarter, ry).start()
        att_side(quarter, 0).start()

    def from_side(*pieces):
        for e in pieces:
            arrived(kv.at[8 + e], kv_recv.at[8 + e])

    def step(i, carry):
        def now(key):
            return sum(jnp.where(i == item, entry, 0) for item, entry in enumerate(key) if entry)

        def event(when, act, *args):
            @pl.when(when)
            def _():
                act(*args)

        first_core, second_core = b == 0, b == 1
        event(jnp.logical_and(i == 0, first_core), take, 1, (2, 3))
        event(i == 0, lambda: [arrived(q_buf.at[pl.ds(n * ROWS, ROWS)], q_recv.at[n]) for n in (0, 3)])
        event(i == 0, far_queries, False)
        event(jnp.logical_and(i == 0, second_core), take, 2, (4,))
        event(i == 0, take, 3)
        event(i == 0, from_side, 0, 1)
        event(i == 1, take, 5, (5,))
        event(i == 1, take, 4)
        event(i == 1, from_side, 2, 3)
        event(i == 2, take, 6)
        event(i == 2, from_side, 4, 5)
        event(i == 3, lambda: arrived(q_buf.at[pl.ds(ROWS, ROWS)], q_recv.at[1]))
        event(i == 3, take, 7)
        event(i == 4, from_side, 6, 7)
        event(i == 5, lambda: arrived(q_buf.at[pl.ds(2 * ROWS, ROWS)], q_recv.at[2]))

        meet(
            [
                keys_step(
                    now([item[s][0] for item in SCHEDULE]),
                    now([item[s][1] for item in SCHEDULE]),
                    now([1 - item[s][0] % 2 for item in SCHEDULE]),
                )
                for s in range(6)
            ]
        )

        event(i == 4, lambda: across_middle([2]))
        event(i == 5, lambda: across_middle([6]))
        event(i == 6, lambda: across_middle([4, 0]))

        @pl.when(i >= 4)
        def _():
            close(now((0, 0, 0, 0, 2, 6, 4, 5)))
            close(now((0, 0, 0, 0, 3, 7, 0, 1)))

        event(i == 7, merge, 2)
        event(i == 7, merge, 3)
        return carry

    lax.fori_loop(0, 8, step, 0)

    def project(quarter):
        slot, h = quarter // 2, quarter % 2
        rows, weights = [], []
        for core in range(2):
            for ry in range(NY):
                t = 1 - b if core else b
                head = (z + NZ - t - 2 * slot) % 4
                place = ry + jnp.where(head // 2 == b, 0, NY)
                rows.append(att[core, quarter, ry])
                weights.append(w_buf[place, pl.ds(pl.multiple_of((head % 2) * HD, HD), HD), :])
        product = lax.dot_general(
            jnp.concatenate(rows, axis=1), jnp.concatenate(weights, axis=0), NN,
            preferred_element_type=jnp.float32,
        )
        here = pl.ds(h * HALF, HALF)
        if slot == 1:
            out_acc[here, :] = product
        else:
            out_ref[here, :] = (out_acc[here, :] + product).astype(out_ref.dtype)

    def gather(quarter):
        for ry in (1, 3, 2):
            arrived(att.at[0, quarter, ry], att_recv.at[0, quarter, ry])
            att_side(quarter, ry).start()

    def finish(quarter):
        for ry in range(NY):
            arrived(att.at[1, quarter, ry], att_recv.at[1, quarter, ry])
        project(quarter)

    for i in range(2):
        for what in range(2):
            sent_unless(*kv_copy(i, what))
            sent_unless(*q_copy(i, what))
    for n in range(1, 2 * NY):
        w_copy(n).wait_send()
    for copy in rings:
        copy.wait_send()
    for e in range(8):
        side_copy(e).wait_send()
    for n in range(2 * NY):
        arrived(w_buf.at[n], w_recv.at[n])
    merge(0)
    gather(2)
    gather(3)
    finish(2)
    merge(1)
    finish(3)
    gather(0)
    gather(1)
    finish(0)
    finish(1)
    for t in range(8):
        sent_unless(*part_copy(t))
    for quarter in range(4):
        for ry in range(1, NY):
            y_copy(quarter, ry).wait_send()
        for ry in range(NY):
            att_side(quarter, ry).wait_send()


def per_device(queries, keys, values, frame_ids, half_order, out_weight):
    hbm = pl.BlockSpec(memory_space=pltpu.HBM)
    smem = pl.BlockSpec(memory_space=pltpu.SMEM)
    bf16, f32 = jnp.bfloat16, jnp.float32
    dma = pltpu.SemaphoreType.DMA
    return pl.pallas_call(
        kernel,
        out_shape=jax.ShapeDtypeStruct((ROWS, COLS), bf16),
        in_specs=[smem, smem, hbm, hbm, hbm, hbm],
        out_specs=pl.BlockSpec(memory_space=pltpu.VMEM),
        scratch_shapes=[
            pltpu.VMEM((4 * ROWS, HD), bf16),
            pltpu.VMEM((16, 2, ROWS, HD), bf16),
            pltpu.VMEM((4 * ROWS, HD), f32),
            pltpu.VMEM((4 * ROWS, HD), f32),
            pltpu.VMEM((4 * ROWS, HD), f32),
            pltpu.VMEM((8, HALF + LOG_ROWS, HD), bf16),
            pltpu.VMEM((4, 2, HALF + LOG_ROWS, HD), bf16),
            pltpu.VMEM((2, 4, NY, HALF, HD), bf16),
            pltpu.VMEM((2 * NY, 2 * HD, COLS), bf16),
            pltpu.VMEM((ROWS, COLS), f32),
            pltpu.SMEM((32,), jnp.int32),
            pltpu.SMEM((8,), jnp.int32),
            pltpu.SMEM((6,), jnp.int32),
            dma((4,)), dma((16,)), dma((4, 2)), dma((2, 4, NY)), dma((2 * NY,)),
            dma((2, 2)), dma((2, 2)), dma((6,)), dma((8,)), dma((2 * NY,)), dma((8,)),
            dma((4, NY - 1)), dma((4, NY)),
        ],
        compiler_params=pltpu.CompilerParams(
            collective_id=0, has_side_effects=True, vmem_limit_bytes=62 * 2**20
        ),
        name="attention_layer",
    )(half_order, frame_ids, queries, keys, values, out_weight)


def solution(mesh):
    placed = (P("ctx", "head"), P("ctx", "head"), P("ctx", "head"), P(), P(), P("head", None))
    return jax.shard_map(
        per_device, mesh=mesh, in_specs=placed, out_specs=P("ctx", "head"), check_vma=False
    )
```
